512 devices in a mesh: batch: 4 (over x_hi, core), space: 128 (over x_lo, z, y).
Axes of the slice: x: 4 (x_hi: 2, x_lo: 2; x = x_hi * 2 + x_lo), y: 4, z: 16, core: 2. Of those that a mesh axis runs over, the one named last changes fastest.
Arguments:
- inputs: bfloat16 [4, 128, 64, 64, 128], P('batch', 'space'), may hold values from -6 to 6
- cotangent: bfloat16 [4, 128, 64, 64, 128], P('batch', 'space'), may hold values from -6 to 6
- mode_weights: bfloat16 [256, 16, 64, 128], P('space'), may hold values from -1.5 to 1.5
Outputs:
- input_grad: bfloat16 [4, 128, 64, 64, 128], P('batch', 'space')
- weight_grad: float32 [256, 16, 64, 128], P('space')
The draws below stay inside these ranges and needn't reach their ends.
All inputs are finite; a program needn't handle non-finite values.
Results may differ from the reference program's by a relative error of at most 0.015.
Values may be sent and summed in bfloat16 or wider, within the bound.
A program may use at most 64 MiB of HBM per device.

```python
import math
import jax
import jax.numpy as jnp
from jax import lax

C = 64
X = 64
Y = 128
Z = 128
MX = 16
MY = 16
MZ = 16
PAIRS = 256
B = 4


def shard_levels(key, shape, pieces, low, high):
    gain, own = 1.0, jax.random.fold_in(key, 6)
    for position, parts in pieces:
        steps = jnp.exp(jax.random.uniform(jax.random.fold_in(own, position), (parts,), jnp.float32, low / len(pieces), high / len(pieces)))
        gain = gain * jnp.repeat(steps, shape[position] // parts).reshape([-1 if axis == position else 1 for axis in range(len(shape))])
    return gain


def bell_draw(key, dims, deviation, bound, pieces=(), kind=jnp.bfloat16):
    gain = shard_levels(key, dims, pieces, -0.22, 0.18) if pieces else 1.0
    array = jax.random.normal(key, dims, jnp.float32) * deviation * gain
    return jnp.minimum(jnp.maximum(array, -bound), bound).astype(kind)


def setup_inputs(seed: int = 0) -> dict:
    splits = jax.random.split(jax.random.key(seed), 4)
    return {
        "inputs": bell_draw(splits[0], (B, Y, C, X, Z), 1.0, 6.0, ((0, 4), (1, 128))),
        "cotangent": bell_draw(splits[1], (B, Y, C, X, Z), 1.0, 6.0, ((0, 4), (1, 128))),
        "mode_weights": bell_draw(splits[2], (PAIRS, MY, C, 2 * C), 0.25, 1.5, ((0, 128),)),
    }


two_pi = 2.0 * math.pi
highest = lax.Precision.HIGHEST

def twiddles(wave_list, positions, length):
    product = wave_list[:, None] * positions[None, :] % length
    angles = two_pi / length * product.astype(jnp.float32)
    return (jnp.cos(angles), jnp.sin(angles))

def wave_pair(retained, length):
    return jnp.concatenate([jnp.arange(retained // 2), jnp.arange(length - retained // 2, length)]).astype(jnp.int32)

def plane_spectrum(values, z_table, cos_x, sin_x, factor):
    lead_dims = values.shape[:-3]
    along_z = jnp.dot(values.reshape(-1, Z), z_table, preferred_element_type=jnp.float32)
    along_z = along_z.reshape(lead_dims + (C, X, 2 * MZ))
    first_term = jnp.einsum('kx,...cxm->...ckm', cos_x, along_z, precision=highest)
    second_term = jnp.einsum('kx,...cxm->...ckm', sin_x, along_z, precision=highest)
    real_part = (first_term[..., :MZ] + second_term[..., MZ:]) * factor
    imag_part = (first_term[..., MZ:] - second_term[..., :MZ]) * factor
    stacked = jnp.stack([real_part, imag_part], axis=-4)
    return stacked.reshape(lead_dims + (2, C, MX * MZ)).astype(jnp.bfloat16)

def modes_along_y(spectra, cos_y, sin_y):
    values_f = spectra.astype(jnp.float32)
    real_in = values_f[:, :, 0]
    imag_in = values_f[:, :, 1]
    real_out = jnp.einsum('ky,bycp->pbkc', cos_y, real_in, precision=highest) + jnp.einsum('ky,bycp->pbkc', sin_y, imag_in, precision=highest)
    imag_out = jnp.einsum('ky,bycp->pbkc', cos_y, imag_in, precision=highest) - jnp.einsum('ky,bycp->pbkc', sin_y, real_in, precision=highest)
    return jnp.stack([real_out, imag_out], axis=3)

def planes_along_y(mode_data, cos_y, sin_y):
    values_f = mode_data.astype(jnp.float32)
    real_in = values_f[:, :, :, 0]
    imag_in = values_f[:, :, :, 1]
    real_out = jnp.einsum('ky,pbkc->bycp', cos_y, real_in, precision=highest) - jnp.einsum('ky,pbkc->bycp', sin_y, imag_in, precision=highest)
    imag_out = jnp.einsum('ky,pbkc->bycp', sin_y, real_in, precision=highest) + jnp.einsum('ky,pbkc->bycp', cos_y, imag_in, precision=highest)
    return jnp.stack([real_out, imag_out], axis=2)

def plane_inverse(spectra, cos_x, sin_x, z_back):
    lead_dims = spectra.shape[:-3]
    values_f = spectra.astype(jnp.float32).reshape(lead_dims + (2, C, MX, MZ))
    real_in = values_f[..., 0, :, :, :]
    imag_in = values_f[..., 1, :, :, :]
    real_out = jnp.einsum('kx,...ckm->...cxm', cos_x, real_in, precision=highest) - jnp.einsum('kx,...ckm->...cxm', sin_x, imag_in, precision=highest)
    imag_out = jnp.einsum('kx,...ckm->...cxm', sin_x, real_in, precision=highest) + jnp.einsum('kx,...ckm->...cxm', cos_x, imag_in, precision=highest)
    joined = jnp.concatenate([real_out, imag_out], axis=-1)
    result = jnp.dot(joined.reshape(-1, 2 * MZ), z_back, precision=highest, preferred_element_type=jnp.float32)
    return result.reshape(lead_dims + (C, X, Z)).astype(jnp.bfloat16)

def split_cot(cot_modes):
    real_part = cot_modes[:, :, :, 0]
    imag_part = cot_modes[:, :, :, 1]
    return (jnp.concatenate([real_part, imag_part], axis=-1), jnp.concatenate([imag_part, -real_part], axis=-1))

def reference(inputs, cotangent, mode_weights):
    inv_scale = 1.0 / math.sqrt(X * Y * Z)
    cos_z, sin_z = twiddles(jnp.arange(MZ).astype(jnp.int32), jnp.arange(Z).astype(jnp.int32), Z)
    z_table = jnp.concatenate([cos_z.T, -sin_z.T], axis=1).astype(jnp.bfloat16)
    z_back = jnp.concatenate([cos_z, -sin_z], axis=0) * inv_scale
    cos_x, sin_x = twiddles(wave_pair(MX, X), jnp.arange(X).astype(jnp.int32), X)
    cos_y, sin_y = twiddles(wave_pair(MY, Y), jnp.arange(Y).astype(jnp.int32), Y)
    plain_z = jnp.full((MZ,), inv_scale, jnp.float32)
    weight_z = jnp.where(jnp.arange(MZ) == 0, 1.0, 2.0).astype(jnp.float32) * inv_scale

    def per_sample(sample):
        values, cot_values = sample
        spec_in = plane_spectrum(values[None], z_table, cos_x, sin_x, plain_z)
        spec_cot = plane_spectrum(cot_values[None], z_table, cos_x, sin_x, weight_z)
        return (modes_along_y(spec_in, cos_y, sin_y)[:, 0], modes_along_y(spec_cot, cos_y, sin_y)[:, 0])
    input_modes, cot_modes = lax.map(per_sample, (inputs, cotangent))
    input_modes = jnp.transpose(input_modes, (1, 0, 2, 3, 4)).astype(jnp.bfloat16)
    cot_modes = jnp.transpose(cot_modes, (1, 0, 2, 3, 4)).astype(jnp.bfloat16)
    cot_one, cot_two = split_cot(cot_modes)
    cot_one = cot_one.astype(jnp.float32)
    cot_two = cot_two.astype(jnp.float32)
    input_f = input_modes.astype(jnp.float32)
    weight_grad = jnp.einsum('pbki,pbkj->pkij', input_f[:, :, :, 0], cot_one) + jnp.einsum('pbki,pbkj->pkij', input_f[:, :, :, 1], cot_two)
    weights_f = mode_weights.astype(jnp.float32)
    grad_real = jnp.einsum('pbkj,pkij->pbki', cot_one, weights_f)
    grad_imag = jnp.einsum('pbkj,pkij->pbki', cot_two, weights_f)
    mode_grad = jnp.stack([grad_real, grad_imag], axis=3).astype(jnp.bfloat16)

    def back_sample(sample_modes):
        planes = planes_along_y(sample_modes[:, None], cos_y, sin_y).astype(jnp.bfloat16)
        return plane_inverse(planes, cos_x, sin_x, z_back)[0]
    input_grad = lax.map(back_sample, jnp.transpose(mode_grad, (1, 0, 2, 3, 4)))
    return (input_grad, weight_grad)
```

```python
import math

import jax
import jax.numpy as jnp
import ml_dtypes
import numpy as np
from jax import lax
from jax.experimental import pallas as pl
from jax.experimental.pallas import tpu as pltpu
from jax.sharding import PartitionSpec as P

C, X, Y, Z = 64, 64, 128, 128
MX, MY, MZ = 16, 16, 16
XL, NZ, NY = 2, 16, 4
NG = XL * NY
NB = 4
MESH = pl.DeviceIdType.MESH
BF, F32 = jnp.bfloat16, jnp.float32

KX = np.concatenate([np.arange(MX // 2), np.arange(X - MX // 2, X)])
KY = np.concatenate([np.arange(MY // 2), np.arange(Y - MY // 2, Y)])
SCALE = 1.0 / math.sqrt(X * Y * Z)


def bf(a):
    return np.asarray(a, np.float64).astype(ml_dtypes.bfloat16)


def turns(k, n, length):
    a = 2.0 * math.pi * ((np.asarray(k)[:, None] * np.asarray(n)[None, :]) % length) / length
    return np.cos(a), np.sin(a)


def tables():
    eye8 = np.eye(8)
    cx, sx = turns(KX, np.arange(X), X)
    ex = np.stack([cx, -sx])
    e8 = np.einsum("pkx,cd->pkcdx", ex, eye8).reshape(2 * MX * 8, 8 * X)
    cz, sz = turns(np.arange(MZ), np.arange(Z), Z)
    tz = np.concatenate(
        [np.concatenate([cz, sz], 1), np.concatenate([-sz, cz], 1)], 0
    )
    a = np.where(np.arange(MZ) == 0, 1.0, 2.0)
    t_in = tz * SCALE
    t_cot = tz * SCALE * np.tile(a, 2)[:, None]
    one_g = np.eye(NG)
    one_e = np.eye(2)
    down, up = [], []
    for g in range(NG):
        cell = 64 * (g // NY) + NY * np.arange(NZ) + g % NY
        cy, sy = turns(KY, cell, Y)
        d = [
            np.einsum("kz,gh,ef->gkezhf", m, one_g, one_e).reshape(256, 256)
            for m in (cy, sy)
        ]
        down.append(np.concatenate([d[0], d[1]], 1))
        up.append(np.concatenate([d[0].T, -d[1].T], 1))
    kz_of = (np.arange(256) // 16 % 2) * 8 + np.arange(256) % 8
    zb = (
        np.concatenate(
            [
                np.concatenate([cz[kz_of], sz[kz_of]], 1),
                np.concatenate([-sz[kz_of], cz[kz_of]], 1),
            ],
            0,
        )
        * SCALE
    )
    return bf(e8), bf(t_in), bf(t_cot), bf(np.stack(down)), bf(np.stack(up)), bf(zb), bf(e8.T)


def swapped(v):
    lane = lax.broadcasted_iota(jnp.int32, v.shape, v.ndim - 1)
    r = pltpu.roll(v, 64, v.ndim - 1)
    return jnp.where(lane < 64, r, -r)


def nn(a, b):
    return lax.dot_general(a, b, (((1,), (0,)), ((), ())), preferred_element_type=F32)


def nt(a, b):
    return lax.dot_general(a, b, (((1,), (1,)), ((), ())), preferred_element_type=F32)


def spectrum(f_ref, sems, copies, e8_ref, t_ref, b_ref, out_ref):
    for i in range(4):
        copies[i].wait()
        lo = f_ref[16 * i : 16 * i + 8].reshape(512, 128)
        hi = f_ref[16 * i + 8 : 16 * i + 16].reshape(512, 128)
        o = nn(e8_ref[...], jnp.concatenate([lo, hi], axis=1)).reshape(32, 8, 256)
        o = jnp.concatenate([o[:, :, :128], o[:, :, 128:]], axis=1)
        b_ref[:, 16 * i : 16 * i + 16, :] = o.astype(BF)
    lane = lax.broadcasted_iota(jnp.int32, (16, 128), 1)
    left = lane < 64
    found = [None] * MX
    for j in range(4):
        re = b_ref[4 * j : 4 * j + 4].reshape(256, 128)
        im = b_ref[16 + 4 * j : 20 + 4 * j].reshape(256, 128)
        o = nt(t_ref[...], jnp.concatenate([re, im], axis=1))
        for h in range(2):
            r = o[:16, 128 * h : 128 * h + 128]
            m = o[16:, 128 * h : 128 * h + 128]
            found[4 * j + 2 * h] = jnp.where(left, r, pltpu.roll(m, 64, 1))
            found[4 * j + 2 * h + 1] = jnp.where(left, pltpu.roll(r, 64, 1), m)
    for z in range(NZ):
        k, h = z // 2, z % 2
        tile = jnp.concatenate(
            [found[k][8 * h : 8 * h + 8], found[8 + k][8 * h : 8 * h + 8]], axis=0
        )
        out_ref[z] = tile.astype(BF)


def main_kernel(
    in_hbm, cot_hbm, w_hbm, e8_hbm, tin_hbm, tcot_hbm, down_hbm, up_hbm,
    q_ref, wg_ref,
    cot_v, in_v, w_v, e8_v, tin_v, tcot_v, down_v, up_v, b_v,
    zs_c, zs_i, zr_c, zr_i, gs_c, gs_i, gr_c, gr_i, du_s, du_r, q_s,
    g_all, u_all,
    load_sem, send_sem, recv_sem,
):
    b = lax.axis_index("batch")
    s = lax.axis_index("space")
    x_lo, z, y = s // (NZ * NY), (s // NY) % NZ, s % NY
    g = x_lo * NY + y

    loads = []

    def load(src, dst):
        c = pltpu.make_async_copy(src, dst, load_sem.at[len(loads)])
        c.start()
        loads.append(c)
        return c

    e8_c = load(e8_hbm, e8_v)
    tcot_c = load(tcot_hbm, tcot_v)
    cot_c = [
        load(cot_hbm.at[0, 0, pl.ds(16 * i, 16)], cot_v.at[pl.ds(16 * i, 16)]) for i in range(4)
    ]
    tin_c = load(tin_hbm, tin_v)
    in_c = [
        load(in_hbm.at[0, 0, pl.ds(16 * i, 16)], in_v.at[pl.ds(16 * i, 16)]) for i in range(4)
    ]
    down_c = load(down_hbm.at[g], down_v)
    w_c = load(w_hbm, w_v)
    up_c = load(up_hbm.at[g], up_v)

    def z_peer(j):
        t = lax.rem(z + j, NZ)
        return t, (b, x_lo * (NZ * NY) + t * NY + y)

    def g_peer(j):
        t = lax.rem(g + j, NG)
        return t, (b, (t // NY) * (NZ * NY) + z * NY + t % NY)

    def b_peer(j):
        return (lax.rem(b + j, NB), s)

    z_order = sorted(range(1, NZ), key=lambda j: -min(j, NZ - j))

    barrier = pltpu.get_barrier_semaphore()
    peers = [z_peer(j)[1] for j in z_order]
    peers += [g_peer(j)[1] for j in range(1, NG)] + [b_peer(j) for j in range(1, NB)]
    for p in peers:
        pl.semaphore_signal(barrier, inc=1, device_id=p, device_id_type=MESH)

    e8_c.wait()
    tcot_c.wait()
    spectrum(cot_v, None, cot_c, e8_v, tcot_v, b_v, zs_c)
    tin_c.wait()
    spectrum(in_v, None, in_c, e8_v, tin_v, b_v, zs_i)
    pl.semaphore_wait(barrier, len(peers))

    def remote(src, dst, k, to):
        pltpu.make_async_remote_copy(
            src_ref=src, dst_ref=dst, send_sem=send_sem.at[k], recv_sem=recv_sem.at[k],
            device_id=to, device_id_type=MESH,
        ).start()

    def z_start(src, dst, k):
        for j in z_order:
            t, to = z_peer(j)
            remote(src.at[t], dst.at[z], k, to)
        pltpu.make_async_copy(src.at[z], dst.at[z], recv_sem.at[k]).start()

    def g_start(src, dst, k):
        for j in range(1, NG):
            t, to = g_peer(j)
            remote(src.at[t], dst.at[g], k, to)
        pltpu.make_async_copy(src.at[g], dst.at[g], recv_sem.at[k]).start()

    def arrived(dst, k):
        pltpu.make_async_copy(dst, dst, recv_sem.at[k]).wait()

    def along_y(table, v):
        v = v.astype(F32)
        both = jnp.concatenate([v.astype(BF), swapped(v).astype(BF)], axis=0)
        return nn(table[...], both)

    z_start(zs_c, zr_c, 0)
    z_start(zs_i, zr_i, 1)

    down_c.wait()
    arrived(zr_c, 0)
    gs_c[...] = along_y(down_v, zr_c[...].reshape(256, 128)).astype(BF).reshape(NG, 32, 128)
    g_start(gs_c, gr_c, 2)
    arrived(zr_i, 1)
    gs_i[...] = along_y(down_v, zr_i[...].reshape(256, 128)).astype(BF).reshape(NG, 32, 128)
    g_start(gs_i, gr_i, 3)

    w_c.wait()
    arrived(gr_c, 2)
    gm = jnp.sum(gr_c[...].astype(F32), axis=0)
    gm_b = gm.astype(BF)
    g_all[b] = gm_b
    gm_f = gm_b.astype(F32)
    both = jnp.concatenate([gm_b, swapped(gm_f).astype(BF)], axis=0)
    row = lax.broadcasted_iota(jnp.int32, (64, 128), 0) % 32
    lane = lax.broadcasted_iota(jnp.int32, (64, 128), 1)
    code = (row % 2) * 16 + row // 2 - lane // 64
    acc = jnp.zeros((64, 128), F32)
    for k in range(8):
        o = nt(both, w_v[k // 4, 4 * (k % 4) : 4 * (k % 4) + 4].reshape(256, 128))
        acc = acc + jnp.where(code == 4 * k, o[:, :128], 0.0)
        acc = acc + jnp.where(code == 4 * k + 2, o[:, 128:], 0.0)
    acc = acc + pltpu.roll(acc, 64, 1)
    du_s[...] = jnp.where(lane[:32] < 64, acc[:32], acc[32:]).astype(BF)
    for j in range(1, NG):
        remote(du_s, du_r.at[g], 4, g_peer(j)[1])
    pltpu.make_async_copy(du_s, du_r.at[g], recv_sem.at[4]).start()
    for j in range(1, NB):
        remote(g_all.at[b], g_all.at[b], 6, b_peer(j))

    arrived(gr_i, 3)
    u_all[b] = jnp.sum(gr_i[...].astype(F32), axis=0).astype(BF)
    for j in range(1, NB):
        remote(u_all.at[b], u_all.at[b], 7, b_peer(j))

    up_c.wait()
    arrived(du_r, 4)
    q_s[...] = along_y(up_v, du_r[...].reshape(256, 128)).astype(BF).reshape(NZ, 16, 128)
    z_start(q_s, q_ref, 5)

    arrived(g_all.at[pl.ds(0, NB - 1)], 6)
    arrived(u_all.at[pl.ds(0, NB - 1)], 7)
    gv = g_all[...].reshape(128, 128)
    rhs = jnp.concatenate([gv, swapped(gv.astype(F32)).astype(BF)], axis=0)
    ut = u_all[...].reshape(128, 128).astype(F32).T
    ut = jnp.concatenate([ut[:64], ut[64:]], axis=1).astype(BF)
    which = lax.broadcasted_iota(jnp.int32, (64, 256), 1) % 32
    for e in range(2):
        for k in range(4):
            lhs = jnp.concatenate(
                [jnp.where(which == 2 * (4 * k + i) + e, ut, jnp.zeros_like(ut)) for i in range(4)],
                axis=0,
            )
            wg_ref[e, 4 * k : 4 * k + 4] = nn(lhs, rhs).reshape(4, 64, 128)

    arrived(q_ref, 5)

    def left(src, k):
        pltpu.make_async_copy(src, src, send_sem.at[k]).wait()

    left(zs_c.at[pl.ds(0, NZ - 1)], 0)
    left(zs_i.at[pl.ds(0, NZ - 1)], 1)
    left(gs_c.at[pl.ds(0, NG - 1)], 2)
    left(gs_i.at[pl.ds(0, NG - 1)], 3)
    left(du_r.at[pl.ds(0, NG - 1)], 4)
    left(q_s.at[pl.ds(0, NZ - 1)], 5)
    left(g_all.at[pl.ds(0, NB - 1)], 6)
    left(u_all.at[pl.ds(0, NB - 1)], 7)


def inverse_kernel(q_ref, wg_ref, zb_ref, xb_ref, ig_hbm, wo_hbm, c_v, o_v, sems):
    wg_c = pltpu.make_async_copy(wg_ref, wo_hbm, sems.at[4])
    wg_c.start()
    qt = q_ref[...].reshape(256, 128).astype(F32).T
    qt = jnp.concatenate([qt[:64], qt[64:]], axis=1).astype(BF)
    at = lax.broadcasted_iota(jnp.int32, (64, 512), 1) % 256
    kx_of = (at // 8 % 2) * 8 + at // 32
    for j in range(4):
        lhs = jnp.concatenate(
            [jnp.where(kx_of == 4 * j + i, qt, jnp.zeros_like(qt)) for i in range(4)], axis=0
        )
        o = nn(lhs, zb_ref[...])
        c_v[4 * j : 4 * j + 4] = o[:, :128].reshape(4, 64, 128)
        c_v[16 + 4 * j : 20 + 4 * j] = o[:, 128:].reshape(4, 64, 128)
    outs = []
    for i in range(4):
        lo = c_v[:, 16 * i : 16 * i + 8].reshape(256, 128)
        hi = c_v[:, 16 * i + 8 : 16 * i + 16].reshape(256, 128)
        o = nn(xb_ref[...], jnp.concatenate([lo, hi], axis=1).astype(BF))
        o_v[16 * i : 16 * i + 8] = o[:, :128].reshape(8, 64, 128).astype(BF)
        o_v[16 * i + 8 : 16 * i + 16] = o[:, 128:].reshape(8, 64, 128).astype(BF)
        c = pltpu.make_async_copy(
            o_v.at[pl.ds(16 * i, 16)], ig_hbm.at[0, 0, pl.ds(16 * i, 16)], sems.at[i]
        )
        c.start()
        outs.append(c)
    for c in outs:
        c.wait()
    wg_c.wait()


def local(inputs, cotangent, mode_weights):
    e8, t_in, t_cot, down, up, zb, xb = (jnp.asarray(t) for t in tables())
    anyw = pl.BlockSpec(memory_space=pltpu.HBM)
    vmem = pl.BlockSpec(memory_space=pltpu.VMEM)
    dma = pltpu.SemaphoreType.DMA
    operands = (inputs, cotangent, mode_weights, e8, t_in, t_cot, down, up)
    q, wg = pl.pallas_call(
        main_kernel,
        out_shape=(
            jax.ShapeDtypeStruct((NZ, 16, 128), BF),
            jax.ShapeDtypeStruct((2, MY, C, 2 * C), F32),
        ),
        in_specs=[anyw] * 8,
        out_specs=(vmem, vmem),
        scratch_shapes=[
            pltpu.VMEM((C, X, Z), BF),
            pltpu.VMEM((C, X, Z), BF),
            pltpu.VMEM((2, MY, C, 2 * C), BF),
            pltpu.VMEM((256, 512), BF),
            pltpu.VMEM((32, 256), BF),
            pltpu.VMEM((32, 256), BF),
            pltpu.VMEM((256, 512), BF),
            pltpu.VMEM((256, 512), BF),
            pltpu.VMEM((2 * MX, C, Z), BF),
            pltpu.VMEM((NZ, 16, 128), BF),
            pltpu.VMEM((NZ, 16, 128), BF),
            pltpu.VMEM((NZ, 16, 128), BF),
            pltpu.VMEM((NZ, 16, 128), BF),
            pltpu.VMEM((NG, 32, 128), BF),
            pltpu.VMEM((NG, 32, 128), BF),
            pltpu.VMEM((NG, 32, 128), BF),
            pltpu.VMEM((NG, 32, 128), BF),
            pltpu.VMEM((32, 128), BF),
            pltpu.VMEM((NG, 32, 128), BF),
            pltpu.VMEM((NZ, 16, 128), BF),
            pltpu.VMEM((NB, 32, 128), BF),
            pltpu.VMEM((NB, 32, 128), BF),
            dma((14,)),
            dma((8,)),
            dma((8,)),
        ],
        compiler_params=pltpu.CompilerParams(
            collective_id=0, has_side_effects=True, vmem_limit_bytes=24 * 2**20
        ),
        cost_estimate=pl.CostEstimate(flops=10**9, bytes_accessed=4 * 2**20, transcendentals=0),
    )(*(pltpu.with_memory_space_constraint(a, pltpu.HBM) for a in operands))
    return pl.pallas_call(
        inverse_kernel,
        out_shape=(
            jax.ShapeDtypeStruct((1, 1, C, X, Z), BF),
            jax.ShapeDtypeStruct((2, MY, C, 2 * C), F32),
        ),
        in_specs=[vmem] * 4,
        out_specs=(anyw, anyw),
        scratch_shapes=[
            pltpu.VMEM((2 * MX, C, Z), F32),
            pltpu.VMEM((C, X, Z), BF),
            dma((5,)),
        ],
        compiler_params=pltpu.CompilerParams(vmem_limit_bytes=16 * 2**20),
        cost_estimate=pl.CostEstimate(flops=10**9, bytes_accessed=4 * 2**20, transcendentals=0),
    )(q, wg, zb, xb)


def solution(mesh):
    placed = (
        P("batch", "space", None, None, None),
        P("batch", "space", None, None, None),
        P("space", None, None, None),
    )
    return jax.shard_map(
        local,
        mesh=mesh,
        in_specs=placed,
        out_specs=(P("batch", "space", None, None, None), P("space", None, None, None)),
        check_vma=False,
    )
```
